32 devices in a mesh: pipe: 8 (over z, x), dp: 4 (over y, core).
Axes of the slice: x: 2, y: 2, z: 4, core: 2. Of those that a mesh axis runs over, the one named last changes fastest.
Arguments:
- parked: bfloat16 [8, 8, 128, 8192], P('pipe', 'dp'), may hold values from -160 to 160
- slot_order: int32 [8, 4, 2], P('pipe', 'dp'), may hold values from 0 to 1, each once within a row
- segment_ids: int32 [8, 8, 128], P('pipe', 'dp'), may hold values from 0 to 3, never falling along the last dimension, each value on 1 to 64 neighbouring positions
- queries: bfloat16 [8, 8, 128, 4096], P('pipe', 'dp'), may hold values from -17 to 17
- out_grad: bfloat16 [8, 8, 128, 4096], P('pipe', 'dp'), may hold values from -4 to 4
- norm_gain: bfloat16 [8, 8192], P('pipe'), may hold values from 0.5 to 1.5
- kv_weight: bfloat16 [8, 8192, 1024], P('pipe', 'dp'), may hold values from -0.0625 to 0.0625
Outputs:
- upstream_grad: bfloat16 [8, 8, 128, 8192], P('pipe', 'dp')
- kv_weight_grad: bfloat16 [8, 8192, 1024], P('pipe', 'dp')
- gain_grad: float32 [8, 8192], P('pipe')
The draws below stay inside these ranges and needn't reach their ends.
All inputs are finite; a program needn't handle non-finite values.
Results may differ from the reference program's by a relative error of at most 0.012.
The reference program's roundings to bfloat16 on the way count: a program that leaves them out, or rounds other values in their place, can miss the bound.
Values may be sent and summed in bfloat16 or wider, within the bound.
A program may use at most 128 MiB of HBM per device.

```python
import math
import jax
import jax.numpy as jnp
import numpy as np
from jax import lax

D = 8192
QH = 32
KVH = 4
HD = 128
S = 128
MB = 2
SECTIONS = 8
REPLICAS = 4
BATCH = 8
KVW = 1024
QW = 4096


def draw_parked(key, part):
    keys = jax.random.split(key, 3)
    shape = (SECTIONS, BATCH, S, D)
    row_scale = jnp.exp(jax.random.uniform(keys[1], (SECTIONS, BATCH, S, 1), jnp.float32, math.log(0.3), math.log(3.0)))
    col_scale = jnp.exp(jax.random.uniform(keys[2], (SECTIONS, 1, 1, D), jnp.float32, math.log(0.5), math.log(5.0)))
    noise = jax.random.truncated_normal(keys[0], -6.0, 6.0, shape, jnp.float32)
    values = row_scale * col_scale * noise
    return values.astype(jnp.bfloat16)


def draw_queries(key, part):
    keys = jax.random.split(key, 1)
    shape = (SECTIONS, BATCH, S, QW)
    values = jax.random.truncated_normal(keys[0], -6.0, 6.0, shape, jnp.float32)
    return values.astype(jnp.bfloat16)


def shard_levels(stream_key, extent, pieces, smallest, largest):
    level, own = 1.0, jax.random.fold_in(stream_key, 6)
    for axis_at, blocks in pieces:
        steps = jnp.exp(jax.random.uniform(jax.random.fold_in(own, axis_at), (blocks,), jnp.float32, smallest / len(pieces), largest / len(pieces)))
        level = level * jnp.repeat(steps, extent[axis_at] // blocks).reshape([-1 if axis == axis_at else 1 for axis in range(len(extent))])
    return level


def profile(amount, total, limit, lean):
    weights = [(1 << 20) // math.isqrt(grade ** lean) + 1 for grade in range(2, amount + 1)]
    rest, holding = total - limit - (amount - 1), [1] * (amount - 1)
    while rest > 0:
        free = [i for i in range(amount - 1) if holding[i] < limit]
        pool, budget = sum([weights[i] for i in free]), rest
        for i in free:
            more = min(limit - holding[i], max(1, budget * weights[i] // pool), rest)
            holding[i] = holding[i] + more
            rest = rest - more
    return np.array([limit] + holding)


def ragged_sizes(rng, count, total, reach, slope):
    if count == 2:
        one = jax.random.randint(rng, (), max(1, total - reach), min(reach, total - 1) + 1)
        return jnp.stack([one, total - one])
    sizes = jnp.asarray(profile(count, total, reach, slope), jnp.int32)
    couples = (count - 1) // 2
    donor, sink = sizes[1:1 + 2 * couples:2], sizes[2:2 + 2 * couples:2]
    margin = jnp.minimum(donor - 1, reach - sink)
    moved = jax.random.randint(jax.random.fold_in(rng, 1), (couples,), 0, 1 << 20) % (margin + 1)
    sizes = sizes.at[1:1 + 2 * couples:2].set(donor - moved).at[2:2 + 2 * couples:2].set(sink + moved)
    return sizes[jax.random.permutation(jax.random.fold_in(rng, 2), count)]


def normal_values(rng, dims, deviation, bound, cuts=(), kind=jnp.bfloat16):
    values = jax.random.normal(rng, dims, jnp.float32) * deviation
    if len(cuts) > 0:
        values = shard_levels(rng, dims, cuts, -0.22, 0.18) * values
    return jnp.clip(values, min=-bound, max=bound).astype(kind)


def setup_inputs(seed: int = 0) -> dict:
    splits = jax.random.split(jax.random.key(seed), 8)
    return {
        "parked": draw_parked(jax.random.fold_in(splits[7], 71), 0),
        "slot_order": jax.vmap(lambda own: jax.random.permutation(own, MB))(jax.random.split(splits[1], SECTIONS * REPLICAS)).reshape((SECTIONS, REPLICAS, MB)).astype(jnp.int32),
        "segment_ids": jax.vmap(lambda own: jnp.searchsorted(jnp.cumsum(ragged_sizes(own, 4, S, S // 2, 1)), jnp.arange(S), side="right"))(jax.random.split(splits[2], SECTIONS * BATCH)).reshape((SECTIONS, BATCH, S)).astype(jnp.int32),
        "queries": draw_queries(jax.random.fold_in(splits[7], 71), 0),
        "out_grad": normal_values(splits[4], (SECTIONS, BATCH, S, QW), 0.25, 4.0, ((0, 8), (1, 4))),
        "norm_gain": jnp.clip(1.0 + 0.1 * jax.random.normal(splits[5], (SECTIONS, D), jnp.float32), 0.5, 1.5).astype(jnp.bfloat16),
        "kv_weight": normal_values(splits[6], (SECTIONS, D, KVW), D ** -0.5, 0.0625, ((0, 8), (1, 4))),
    }


EPSILON = 1e-05

def attention_grads(queries, out_grad, keys, values, segments):
    batch_count = queries.shape[0]
    seq_len = queries.shape[1]
    group_size = QH // KVH
    scaling = 1.0 / math.sqrt(HD)
    query_heads = queries.astype(jnp.float32).reshape(batch_count, seq_len, KVH, group_size, HD)
    grad_heads = out_grad.astype(jnp.float32).reshape(batch_count, seq_len, KVH, group_size, HD)
    key_heads = keys.astype(jnp.float32).reshape(batch_count, seq_len, KVH, HD)
    value_heads = values.astype(jnp.float32).reshape(batch_count, seq_len, KVH, HD)
    scores = jnp.einsum('bqhgd,bkhd->bhgqk', query_heads, key_heads) * scaling
    position = jnp.arange(seq_len)
    causal = position[None, :] <= position[:, None]
    allowed = causal[None] & (segments[:, :, None] == segments[:, None, :])
    scores = jnp.where(allowed[:, None, None], scores, -1e+30)
    highest = lax.optimization_barrier(jnp.max(scores, axis=-1, keepdims=True))
    weights = jnp.exp(scores - highest)
    probabilities = weights / lax.optimization_barrier(jnp.sum(weights, axis=-1, keepdims=True))
    probs_low = probabilities.astype(jnp.bfloat16)
    value_grad = jnp.einsum('bhgqk,bqhgd->bkhd', probs_low.astype(jnp.float32), grad_heads)
    prob_grad = jnp.einsum('bqhgd,bkhd->bhgqk', grad_heads, value_heads)
    row_dot = lax.optimization_barrier(jnp.sum(probabilities * prob_grad, axis=-1, keepdims=True))
    score_grad = (probabilities * (prob_grad - row_dot) * scaling).astype(jnp.bfloat16)
    key_grad = jnp.einsum('bhgqk,bqhgd->bkhd', score_grad.astype(jnp.float32), query_heads)
    key_low = key_grad.astype(jnp.bfloat16).reshape(batch_count, seq_len, KVH * HD)
    value_low = value_grad.astype(jnp.bfloat16).reshape(batch_count, seq_len, KVH * HD)
    return jnp.concatenate([key_low, value_low], axis=-1)

def reference(parked, slot_order, segment_ids, queries, out_grad, norm_gain, kv_weight):

    def one_section(section_index):
        source = parked[SECTIONS - 1 - section_index]
        slot_rows = (jnp.arange(REPLICAS, dtype=jnp.int32)[:, None] * MB + slot_order[section_index]).reshape(-1).astype(jnp.int32)
        inputs = jnp.take(source, slot_rows, axis=0)
        inputs_wide = inputs.astype(jnp.float32)
        inverse = lax.rsqrt(lax.optimization_barrier(jnp.mean(inputs_wide * inputs_wide, axis=-1)) + EPSILON)
        scale_col = inverse[..., None]
        gain_full = norm_gain[section_index].astype(jnp.float32)
        normed = (inputs_wide * scale_col * gain_full).astype(jnp.bfloat16)
        weight = kv_weight[section_index]
        flat_normed = normed.reshape(BATCH * S, D)
        projected = jnp.dot(flat_normed, weight, preferred_element_type=jnp.float32).astype(jnp.bfloat16)
        projected = projected.reshape(BATCH, S, KVW)
        head_span = KVH * HD
        kv_grads = attention_grads(queries[section_index], out_grad[section_index], projected[..., :head_span], projected[..., head_span:], segment_ids[section_index])
        flat_grads = kv_grads.reshape(BATCH * S, KVW)
        weight_grad = lax.dot_general(flat_normed, flat_grads, (((0,), (0,)), ((), ())), preferred_element_type=jnp.float32).astype(jnp.bfloat16)
        normed_grad = lax.dot_general(flat_grads, weight, (((1,), (1,)), ((), ())), preferred_element_type=jnp.float32).reshape(BATCH, S, D)
        scaled_grad = normed_grad * gain_full
        inner_mean = lax.optimization_barrier(jnp.mean(scaled_grad * inputs_wide, axis=-1, keepdims=True))
        input_grad = (scale_col * scaled_grad - inputs_wide * scale_col ** 3 * inner_mean).astype(jnp.bfloat16)
        gain_grad = lax.optimization_barrier(jnp.sum(normed_grad * inputs_wide * scale_col, axis=(0, 1)))
        return (input_grad, weight_grad, gain_grad)
    input_grads, weight_grads, gain_grads = lax.map(one_section, jnp.arange(SECTIONS, dtype=jnp.int32))
    upstream_grad = jnp.concatenate([input_grads[1:], jnp.zeros_like(input_grads[:1])], axis=0)
    return (upstream_grad, weight_grads, gain_grads)
```

```python
import math

import jax
import jax.numpy as jnp
from jax import lax
from jax.sharding import PartitionSpec as P

QH = 32
KVH = 4
HD = 128


EPSILON = 1e-05


def shifted(value, axis, steps):
    count = lax.axis_size(axis)
    leading, last = (max(0, -steps), min(count, count - steps))
    return lax.ppermute(value, axis, [(source, source + steps) for source in range(leading, last)])


def mirrored(value, axis):
    count = lax.axis_size(axis)
    return lax.ppermute(value, axis, [(source, count - 1 - source) for source in range(count)])


def attention_grads(queries, out_grad, keys, values, segments):
    seq_len = queries.shape[0]
    group_size = QH // KVH
    scaling = 1.0 / math.sqrt(HD)
    query_heads = queries.reshape(seq_len, KVH, group_size, HD)
    grad_heads = out_grad.reshape(seq_len, KVH, group_size, HD)
    key_heads = keys.reshape(seq_len, KVH, HD)
    value_heads = values.reshape(seq_len, KVH, HD)
    scores = (
        jnp.einsum("qhgd,khd->hgqk", query_heads, key_heads, preferred_element_type=jnp.float32)
        * scaling
    )
    position = jnp.arange(seq_len)
    causal = position[None, :] <= position[:, None]
    allowed = causal & (segments[:, None] == segments[None, :])
    scores = jnp.where(allowed[None, None], scores, -1e30)
    highest = jnp.max(scores, axis=-1, keepdims=True)
    weights = jnp.exp(scores - highest)
    probabilities = weights / jnp.sum(weights, axis=-1, keepdims=True)
    probs_low = probabilities.astype(jnp.bfloat16)
    value_grad = jnp.einsum(
        "hgqk,qhgd->khd", probs_low, grad_heads, preferred_element_type=jnp.float32
    )
    prob_grad = jnp.einsum(
        "qhgd,khd->hgqk", grad_heads, value_heads, preferred_element_type=jnp.float32
    )
    row_dot = jnp.sum(probabilities * prob_grad, axis=-1, keepdims=True)
    score_grad = (probabilities * (prob_grad - row_dot) * scaling).astype(jnp.bfloat16)
    key_grad = jnp.einsum(
        "hgqk,qhgd->khd", score_grad, query_heads, preferred_element_type=jnp.float32
    )
    key_low = key_grad.astype(jnp.bfloat16).reshape(seq_len, KVH * HD)
    value_low = value_grad.astype(jnp.bfloat16).reshape(seq_len, KVH * HD)
    return jnp.concatenate([key_low, value_low], axis=-1)


def local(parked, slot_order, segment_ids, queries, out_grad, norm_gain, kv_weight):
    stored = parked[0]
    order = slot_order[0, 0]
    micro_count, seq_len, feature_count = stored.shape
    gain_full = norm_gain[0].astype(jnp.float32)
    local_weight = kv_weight[0]
    slice_width = local_weight.shape[0]
    start_col = lax.axis_index("dp") * slice_width
    gain_local = lax.dynamic_slice_in_dim(gain_full, start_col, slice_width)
    full_weight = lax.all_gather(local_weight, "dp", axis=0, tiled=True)
    order_next = shifted(order, "pipe", -1)

    arrived = []
    for slot in range(micro_count):
        block = stored[slot]
        if arrived:
            arrived[-1], block = lax.optimization_barrier((arrived[-1], block))
        arrived.append(mirrored(block, "pipe"))

    all_normed, all_grads, shifts = [], [], []
    for slot in range(micro_count):
        micro = jnp.argmax(order == slot)
        inputs_wide = arrived[slot].astype(jnp.float32)
        inverse = lax.rsqrt(jnp.mean(inputs_wide * inputs_wide, axis=-1, keepdims=True) + EPSILON)
        normed = (inputs_wide * inverse * gain_full).astype(jnp.bfloat16)
        all_normed.append(lax.all_to_all(normed, "dp", split_axis=1, concat_axis=0, tiled=True))
        projected = jnp.dot(normed, full_weight, preferred_element_type=jnp.float32)
        projected_low = projected.astype(jnp.bfloat16)
        head_span = projected_low.shape[-1] // 2
        kv_grads = attention_grads(
            lax.dynamic_index_in_dim(queries[0], micro, keepdims=False),
            lax.dynamic_index_in_dim(out_grad[0], micro, keepdims=False),
            projected_low[..., :head_span],
            projected_low[..., head_span:],
            lax.dynamic_index_in_dim(segment_ids[0], micro, keepdims=False),
        )
        all_grads.append(lax.all_gather(kv_grads, "dp", axis=0, tiled=True))
        inner = jnp.sum(kv_grads.astype(jnp.float32) * projected, axis=-1, keepdims=True)
        inner = inner * (inverse * inverse / feature_count)
        normed_grad = lax.dot_general(
            kv_grads, full_weight, (((1,), (1,)), ((), ())), preferred_element_type=jnp.float32
        )
        input_grad = (inverse * gain_full * normed_grad - inputs_wide * inner).astype(jnp.bfloat16)
        shifts.append(shifted(input_grad, "pipe", -1))
        if slot + 1 < micro_count:
            arrived[slot + 1], _ = lax.optimization_barrier((arrived[slot + 1], input_grad))

    weight_wide = lax.dot_general(
        jnp.concatenate(all_normed),
        jnp.concatenate(all_grads),
        (((0,), (0,)), ((), ())),
        preferred_element_type=jnp.float32,
    )
    gain_part = jnp.sum(weight_wide * local_weight.astype(jnp.float32), axis=-1) / gain_local
    gain_grad = lax.all_gather(gain_part, "dp", axis=0, tiled=True)
    upstream = jnp.zeros((micro_count, seq_len, feature_count), jnp.bfloat16)
    for slot in range(micro_count):
        upstream = lax.dynamic_update_index_in_dim(
            upstream, shifts[slot], jnp.argmax(order_next == slot), 0
        )
    return (upstream[None], weight_wide.astype(jnp.bfloat16)[None], gain_grad[None])


def solution(mesh):
    return jax.shard_map(
        local,
        mesh=mesh,
        in_specs=(
            P("pipe", "dp", None, None),
            P("pipe", "dp", None),
            P("pipe", "dp", None),
            P("pipe", "dp", None, None),
            P("pipe", "dp", None, None),
            P("pipe", None),
            P("pipe", "dp", None),
        ),
        out_specs=(P("pipe", "dp", None, None), P("pipe", "dp", None), P("pipe", None)),
        check_vma=False,
    )
```

```python
import math

import jax
import jax.numpy as jnp
from jax import lax
from jax.sharding import PartitionSpec as P

QH = 32
KVH = 4
HD = 128


EPSILON = 1e-05


def shifted(value, axis, steps):
    count = lax.axis_size(axis)
    leading, last = (max(0, -steps), min(count, count - steps))
    return lax.ppermute(value, axis, [(source, source + steps) for source in range(leading, last)])


def mirrored(value, axis):
    count = lax.axis_size(axis)
    return lax.ppermute(value, axis, [(source, count - 1 - source) for source in range(count)])


def attention_grads(queries, out_grad, keys, values, segments):
    seq_len = queries.shape[0]
    group_size = QH // KVH
    scaling = 1.0 / math.sqrt(HD)
    query_heads = queries.reshape(seq_len, KVH, group_size, HD)
    grad_heads = out_grad.reshape(seq_len, KVH, group_size, HD)
    key_heads = keys.reshape(seq_len, KVH, HD)
    value_heads = values.reshape(seq_len, KVH, HD)
    scores = (
        jnp.einsum("qhgd,khd->hgqk", query_heads, key_heads, preferred_element_type=jnp.float32)
        * scaling
    )
    position = jnp.arange(seq_len)
    causal = position[None, :] <= position[:, None]
    allowed = causal & (segments[:, None] == segments[None, :])
    scores = jnp.where(allowed[None, None], scores, -1e30)
    highest = jnp.max(scores, axis=-1, keepdims=True)
    weights = jnp.exp(scores - highest)
    probabilities = weights / jnp.sum(weights, axis=-1, keepdims=True)
    probs_low = probabilities.astype(jnp.bfloat16)
    value_grad = jnp.einsum(
        "hgqk,qhgd->khd", probs_low, grad_heads, preferred_element_type=jnp.float32
    )
    prob_grad = jnp.einsum(
        "qhgd,khd->hgqk", grad_heads, value_heads, preferred_element_type=jnp.float32
    )
    row_dot = jnp.sum(probabilities * prob_grad, axis=-1, keepdims=True)
    score_grad = (probabilities * (prob_grad - row_dot) * scaling).astype(jnp.bfloat16)
    key_grad = jnp.einsum(
        "hgqk,qhgd->khd", score_grad, query_heads, preferred_element_type=jnp.float32
    )
    key_low = key_grad.astype(jnp.bfloat16).reshape(seq_len, KVH * HD)
    value_low = value_grad.astype(jnp.bfloat16).reshape(seq_len, KVH * HD)
    return jnp.concatenate([key_low, value_low], axis=-1)


def local(parked, slot_order, segment_ids, queries, out_grad, norm_gain, kv_weight):
    stored = parked[0]
    order = slot_order[0, 0]
    micro_count, seq_len, feature_count = stored.shape
    gain_full = norm_gain[0].astype(jnp.float32)
    local_weight = kv_weight[0]
    slice_width = local_weight.shape[0]
    start_col = lax.axis_index("dp") * slice_width
    gain_local = lax.dynamic_slice_in_dim(gain_full, start_col, slice_width)
    full_weight = lax.all_gather(local_weight, "dp", axis=0, tiled=True)
    order_next = shifted(order, "pipe", -1)

    arrived = []
    for slot in range(micro_count):
        block = stored[slot]
        if arrived:
            arrived[-1], block = lax.optimization_barrier((arrived[-1], block))
        arrived.append(mirrored(block, "pipe"))

    all_normed, all_grads, shifts = [], [], []
    for slot in range(micro_count):
        micro = jnp.argmax(order == slot)
        inputs_wide = arrived[slot].astype(jnp.float32)
        inverse = lax.rsqrt(jnp.mean(inputs_wide * inputs_wide, axis=-1, keepdims=True) + EPSILON)
        normed = (inputs_wide * inverse * gain_full).astype(jnp.bfloat16)
        all_normed.append(lax.all_to_all(normed, "dp", split_axis=1, concat_axis=0, tiled=True))
        projected = jnp.dot(normed, full_weight, preferred_element_type=jnp.float32)
        projected_low = projected.astype(jnp.bfloat16)
        head_span = projected_low.shape[-1] // 2
        kv_grads = attention_grads(
            lax.dynamic_index_in_dim(queries[0], micro, keepdims=False),
            lax.dynamic_index_in_dim(out_grad[0], micro, keepdims=False),
            projected_low[..., :head_span],
            projected_low[..., head_span:],
            lax.dynamic_index_in_dim(segment_ids[0], micro, keepdims=False),
        )
        all_grads.append(lax.all_gather(kv_grads, "dp", axis=0, tiled=True))
        if shifts:
            kv_grads, shifts[-1] = lax.optimization_barrier((kv_grads, shifts[-1]))
        inner = jnp.sum(kv_grads.astype(jnp.float32) * projected, axis=-1, keepdims=True)
        inner = inner * (inverse * inverse / feature_count)
        normed_grad = lax.dot_general(
            kv_grads, full_weight, (((1,), (1,)), ((), ())), preferred_element_type=jnp.float32
        )
        input_grad = (inverse * gain_full * normed_grad - inputs_wide * inner).astype(jnp.bfloat16)
        shifts.append(shifted(input_grad, "pipe", -1))
        if slot + 1 < micro_count:
            arrived[slot + 1], _ = lax.optimization_barrier((arrived[slot + 1], input_grad))

    weight_wide = lax.dot_general(
        jnp.concatenate(all_normed),
        jnp.concatenate(all_grads),
        (((0,), (0,)), ((), ())),
        preferred_element_type=jnp.float32,
    )
    gain_part = jnp.sum(weight_wide * local_weight.astype(jnp.float32), axis=-1) / gain_local
    gain_grad = lax.all_gather(gain_part, "dp", axis=0, tiled=True)
    upstream = jnp.zeros((micro_count, seq_len, feature_count), jnp.bfloat16)
    for slot in range(micro_count):
        upstream = lax.dynamic_update_index_in_dim(
            upstream, shifts[slot], jnp.argmax(order_next == slot), 0
        )
    return (upstream[None], weight_wide.astype(jnp.bfloat16)[None], gain_grad[None])


def solution(mesh):
    return jax.shard_map(
        local,
        mesh=mesh,
        in_specs=(
            P("pipe", "dp", None, None),
            P("pipe", "dp", None),
            P("pipe", "dp", None),
            P("pipe", "dp", None, None),
            P("pipe", "dp", None, None),
            P("pipe", None),
            P("pipe", "dp", None),
        ),
        out_specs=(P("pipe", "dp", None, None), P("pipe", "dp", None), P("pipe", None)),
        check_vma=False,
    )
```

```python
import math

import jax
import jax.numpy as jnp
from jax import lax
from jax.sharding import PartitionSpec as P

QH = 32
KVH = 4
HD = 128


EPSILON = 1e-05


def shifted(value, axis, steps):
    count = lax.axis_size(axis)
    leading, last = (max(0, -steps), min(count, count - steps))
    return lax.ppermute(value, axis, [(source, source + steps) for source in range(leading, last)])


def mirrored(value, axis):
    count = lax.axis_size(axis)
    return lax.ppermute(value, axis, [(source, count - 1 - source) for source in range(count)])


def attention_grads(queries, out_grad, keys, values, segments):
    seq_len = queries.shape[0]
    group_size = QH // KVH
    scaling = 1.0 / math.sqrt(HD)
    query_heads = queries.reshape(seq_len, KVH, group_size, HD)
    grad_heads = out_grad.reshape(seq_len, KVH, group_size, HD)
    key_heads = keys.reshape(seq_len, KVH, HD)
    value_heads = values.reshape(seq_len, KVH, HD)
    scores = (
        jnp.einsum("qhgd,khd->hgqk", query_heads, key_heads, preferred_element_type=jnp.float32)
        * scaling
    )
    position = jnp.arange(seq_len)
    causal = position[None, :] <= position[:, None]
    allowed = causal & (segments[:, None] == segments[None, :])
    scores = jnp.where(allowed[None, None], scores, -1e30)
    highest = jnp.max(scores, axis=-1, keepdims=True)
    weights = jnp.exp(scores - highest)
    probabilities = weights / jnp.sum(weights, axis=-1, keepdims=True)
    probs_low = probabilities.astype(jnp.bfloat16)
    value_grad = jnp.einsum(
        "hgqk,qhgd->khd", probs_low, grad_heads, preferred_element_type=jnp.float32
    )
    prob_grad = jnp.einsum(
        "qhgd,khd->hgqk", grad_heads, value_heads, preferred_element_type=jnp.float32
    )
    row_dot = jnp.sum(probabilities * prob_grad, axis=-1, keepdims=True)
    score_grad = (probabilities * (prob_grad - row_dot) * scaling).astype(jnp.bfloat16)
    key_grad = jnp.einsum(
        "hgqk,qhgd->khd", score_grad, query_heads, preferred_element_type=jnp.float32
    )
    key_low = key_grad.astype(jnp.bfloat16).reshape(seq_len, KVH * HD)
    value_low = value_grad.astype(jnp.bfloat16).reshape(seq_len, KVH * HD)
    return jnp.concatenate([key_low, value_low], axis=-1)


def local(parked, slot_order, segment_ids, queries, out_grad, norm_gain, kv_weight):
    stored = parked[0]
    order = slot_order[0, 0]
    micro_count, seq_len, feature_count = stored.shape
    gain_full = norm_gain[0].astype(jnp.float32)
    local_weight = kv_weight[0]
    slice_width = local_weight.shape[0]
    start_col = lax.axis_index("dp") * slice_width
    gain_local = lax.dynamic_slice_in_dim(gain_full, start_col, slice_width)
    full_weight = lax.all_gather(local_weight, "dp", axis=0, tiled=True)
    order_next = shifted(order, "pipe", -1)

    arrived = []
    for slot in range(micro_count):
        block = stored[slot]
        if arrived:
            arrived[-1], block = lax.optimization_barrier((arrived[-1], block))
        arrived.append(mirrored(block, "pipe"))

    all_normed, all_grads, shifts = [], [], []
    for slot in range(micro_count):
        micro = jnp.argmax(order == slot)
        inputs_wide = arrived[slot].astype(jnp.float32)
        inverse = lax.rsqrt(jnp.mean(inputs_wide * inputs_wide, axis=-1, keepdims=True) + EPSILON)
        normed = (inputs_wide * inverse * gain_full).astype(jnp.bfloat16)
        sent, _ = lax.optimization_barrier((normed, full_weight))
        all_normed.append(lax.all_to_all(sent, "dp", split_axis=1, concat_axis=0, tiled=True))
        projected = jnp.dot(normed, full_weight, preferred_element_type=jnp.float32)
        projected_low = projected.astype(jnp.bfloat16)
        head_span = projected_low.shape[-1] // 2
        kv_grads = attention_grads(
            lax.dynamic_index_in_dim(queries[0], micro, keepdims=False),
            lax.dynamic_index_in_dim(out_grad[0], micro, keepdims=False),
            projected_low[..., :head_span],
            projected_low[..., head_span:],
            lax.dynamic_index_in_dim(segment_ids[0], micro, keepdims=False),
        )
        all_grads.append(lax.all_gather(kv_grads, "dp", axis=0, tiled=True))
        if shifts:
            kv_grads, shifts[-1] = lax.optimization_barrier((kv_grads, shifts[-1]))
        inner = jnp.sum(kv_grads.astype(jnp.float32) * projected, axis=-1, keepdims=True)
        inner = inner * (inverse * inverse / feature_count)
        normed_grad = lax.dot_general(
            kv_grads, full_weight, (((1,), (1,)), ((), ())), preferred_element_type=jnp.float32
        )
        input_grad = (inverse * gain_full * normed_grad - inputs_wide * inner).astype(jnp.bfloat16)
        shifts.append(shifted(input_grad, "pipe", -1))
        if slot + 1 < micro_count:
            arrived[slot + 1], _ = lax.optimization_barrier((arrived[slot + 1], input_grad))

    weight_wide = lax.dot_general(
        jnp.concatenate(all_normed),
        jnp.concatenate(all_grads),
        (((0,), (0,)), ((), ())),
        preferred_element_type=jnp.float32,
    )
    gain_part = jnp.sum(weight_wide * local_weight.astype(jnp.float32), axis=-1) / gain_local
    gain_grad = lax.all_gather(gain_part, "dp", axis=0, tiled=True)
    upstream = jnp.zeros((micro_count, seq_len, feature_count), jnp.bfloat16)
    for slot in range(micro_count):
        upstream = lax.dynamic_update_index_in_dim(
            upstream, shifts[slot], jnp.argmax(order_next == slot), 0
        )
    return (upstream[None], weight_wide.astype(jnp.bfloat16)[None], gain_grad[None])


def solution(mesh):
    return jax.shard_map(
        local,
        mesh=mesh,
        in_specs=(
            P("pipe", "dp", None, None),
            P("pipe", "dp", None),
            P("pipe", "dp", None),
            P("pipe", "dp", None, None),
            P("pipe", "dp", None, None),
            P("pipe", None),
            P("pipe", "dp", None),
        ),
        out_specs=(P("pipe", "dp", None, None), P("pipe", "dp", None), P("pipe", None)),
        check_vma=False,
    )
```

```python
import math

import jax
import jax.numpy as jnp
from jax import lax
from jax.sharding import PartitionSpec as P

QH = 32
KVH = 4
HD = 128


EPSILON = 1e-05


def shifted(value, axis, steps):
    count = lax.axis_size(axis)
    leading, last = (max(0, -steps), min(count, count - steps))
    return lax.ppermute(value, axis, [(source, source + steps) for source in range(leading, last)])


def mirrored(value, axis):
    count = lax.axis_size(axis)
    return lax.ppermute(value, axis, [(source, count - 1 - source) for source in range(count)])


def attention_grads(queries, out_grad, keys, values, segments):
    seq_len = queries.shape[0]
    group_size = QH // KVH
    scaling = 1.0 / math.sqrt(HD)
    query_heads = queries.reshape(seq_len, KVH, group_size, HD)
    grad_heads = out_grad.reshape(seq_len, KVH, group_size, HD)
    key_heads = keys.reshape(seq_len, KVH, HD)
    value_heads = values.reshape(seq_len, KVH, HD)
    scores = (
        jnp.einsum("qhgd,khd->hgqk", query_heads, key_heads, preferred_element_type=jnp.float32)
        * scaling
    )
    position = jnp.arange(seq_len)
    causal = position[None, :] <= position[:, None]
    allowed = causal & (segments[:, None] == segments[None, :])
    scores = jnp.where(allowed[None, None], scores, -1e30)
    highest = jnp.max(scores, axis=-1, keepdims=True)
    weights = jnp.exp(scores - highest)
    probabilities = weights / jnp.sum(weights, axis=-1, keepdims=True)
    probs_low = probabilities.astype(jnp.bfloat16)
    value_grad = jnp.einsum(
        "hgqk,qhgd->khd", probs_low, grad_heads, preferred_element_type=jnp.float32
    )
    prob_grad = jnp.einsum(
        "qhgd,khd->hgqk", grad_heads, value_heads, preferred_element_type=jnp.float32
    )
    row_dot = jnp.sum(probabilities * prob_grad, axis=-1, keepdims=True)
    score_grad = (probabilities * (prob_grad - row_dot) * scaling).astype(jnp.bfloat16)
    key_grad = jnp.einsum(
        "hgqk,qhgd->khd", score_grad, query_heads, preferred_element_type=jnp.float32
    )
    key_low = key_grad.astype(jnp.bfloat16).reshape(seq_len, KVH * HD)
    value_low = value_grad.astype(jnp.bfloat16).reshape(seq_len, KVH * HD)
    return jnp.concatenate([key_low, value_low], axis=-1)


def local(parked, slot_order, segment_ids, queries, out_grad, norm_gain, kv_weight):
    stored = parked[0]
    order = slot_order[0, 0]
    micro_count, seq_len, feature_count = stored.shape
    gain_full = norm_gain[0].astype(jnp.float32)
    local_weight = kv_weight[0]
    slice_width = local_weight.shape[0]
    start_col = lax.axis_index("dp") * slice_width
    gain_local = lax.dynamic_slice_in_dim(gain_full, start_col, slice_width)
    full_weight = lax.all_gather(local_weight, "dp", axis=0, tiled=True)
    order_next = shifted(order, "pipe", -1)

    arrived = []
    for slot in range(micro_count):
        block = stored[slot]
        if arrived:
            arrived[-1], block = lax.optimization_barrier((arrived[-1], block))
        arrived.append(mirrored(block, "pipe"))

    all_normed, all_grads, shifts, places = [], [], [], []
    for slot in range(micro_count):
        micro = jnp.argmax(order == slot)
        inputs_wide = arrived[slot].astype(jnp.float32)
        inverse = lax.rsqrt(jnp.mean(inputs_wide * inputs_wide, axis=-1, keepdims=True) + EPSILON)
        normed = (inputs_wide * inverse * gain_full).astype(jnp.bfloat16)
        sent, _ = lax.optimization_barrier((normed, full_weight))
        all_normed.append(lax.all_to_all(sent, "dp", split_axis=1, concat_axis=0, tiled=True))
        projected = jnp.dot(normed, full_weight, preferred_element_type=jnp.float32)
        projected_low = projected.astype(jnp.bfloat16)
        head_span = projected_low.shape[-1] // 2
        kv_grads = attention_grads(
            lax.dynamic_index_in_dim(queries[0], micro, keepdims=False),
            lax.dynamic_index_in_dim(out_grad[0], micro, keepdims=False),
            projected_low[..., :head_span],
            projected_low[..., head_span:],
            lax.dynamic_index_in_dim(segment_ids[0], micro, keepdims=False),
        )
        all_grads.append(lax.all_gather(kv_grads, "dp", axis=0, tiled=True))
        inner = jnp.sum(kv_grads.astype(jnp.float32) * projected, axis=-1, keepdims=True)
        inner = inner * (inverse * inverse / feature_count)
        pieces = 1 if slot + 1 < micro_count else 2
        width = feature_count // pieces
        for piece in range(pieces):
            if piece and len(shifts) > piece:
                kv_grads, shifts[0], all_normed[-1] = lax.optimization_barrier(
                    (kv_grads, shifts[0], all_normed[-1])
                )
            span = slice(piece * width, (piece + 1) * width)
            normed_grad = lax.dot_general(
                kv_grads,
                full_weight[span],
                (((1,), (1,)), ((), ())),
                preferred_element_type=jnp.float32,
            )
            input_grad = (
                inverse * gain_full[span] * normed_grad - inputs_wide[:, span] * inner
            ).astype(jnp.bfloat16)
            shifts.append(shifted(input_grad, "pipe", -1))
            places.append((slot, piece * width))
        if slot + 1 < micro_count:
            arrived[slot + 1], _ = lax.optimization_barrier((arrived[slot + 1], input_grad))

    weight_wide = lax.dot_general(
        jnp.concatenate(all_normed),
        jnp.concatenate(all_grads),
        (((0,), (0,)), ((), ())),
        preferred_element_type=jnp.float32,
    )
    gain_part = jnp.sum(weight_wide * local_weight.astype(jnp.float32), axis=-1) / gain_local
    gain_grad = lax.all_gather(gain_part, "dp", axis=0, tiled=True)
    upstream = jnp.zeros((micro_count, seq_len, feature_count), jnp.bfloat16)
    for moved, (slot, column) in zip(shifts, places):
        upstream = lax.dynamic_update_slice(
            upstream, moved[None], (jnp.argmax(order_next == slot), 0, column)
        )
    return (upstream[None], weight_wide.astype(jnp.bfloat16)[None], gain_grad[None])


def solution(mesh):
    return jax.shard_map(
        local,
        mesh=mesh,
        in_specs=(
            P("pipe", "dp", None, None),
            P("pipe", "dp", None),
            P("pipe", "dp", None),
            P("pipe", "dp", None, None),
            P("pipe", "dp", None, None),
            P("pipe", None),
            P("pipe", "dp", None),
        ),
        out_specs=(P("pipe", "dp", None, None), P("pipe", "dp", None), P("pipe", None)),
        check_vma=False,
    )
```
